32 devices in a mesh: prow: 8 (over z, y), pcol: 4 (over x, core).
Axes of the slice: x: 2, y: 2, z: 4, core: 2. Of those that a mesh axis runs over, the one named last changes fastest.
Arguments:
- matrix: bfloat16 [14336, 7168], P('prow', 'pcol'), may hold values from -6 to 6
- pivots: int32 [256], replicated, may hold values from 0 to 14335
Outputs:
- factored: bfloat16 [14336, 7168], P('prow', 'pcol')
The draws below stay inside these ranges and needn't reach their ends.
All inputs are finite; a program needn't handle non-finite values.
Results may differ from the reference program's by a relative error of at most 0.0044.
Values may be sent and summed in bfloat16 or wider, within the bound.
No kernel may reach another device: no remote copies, remote signals or barrier semaphores. Data moves between devices by JAX's collectives and lax.ppermute only.
A program may use at most 64 MiB of HBM per device.

```python
import jax
import jax.numpy as jnp
from jax import lax

NB = 256
RLOC = 1792
NROWS = 14336
NCOLS = 7168
N_PROW = 8


def draw_matrix(key, part):
    key_values = jax.random.fold_in(key, 0)
    values = jnp.clip(jax.random.normal(key_values, (NROWS, NCOLS), jnp.float32), -6.0, 6.0)
    columns = jnp.arange(NCOLS)[None, :]
    factor = jnp.where(columns < NB, NB ** (-0.5), 1.0)
    return (values * factor).astype(jnp.bfloat16)


def draw_pivots(key, part):
    return jax.random.randint(key, (NB,), jnp.arange(NB, dtype=jnp.int32), NROWS, dtype=jnp.int32)


def setup_inputs(seed: int = 0) -> dict:
    streams_of = jax.random.split(jax.random.key(seed), 3)
    matrix = draw_matrix(jax.random.fold_in(streams_of[2], 71), 0)
    pivots = draw_pivots(jax.random.fold_in(streams_of[2], 71), 0)
    return {"matrix": matrix, "pivots": pivots}


def storage(global_row):
    block_index = global_row // NB
    return block_index % N_PROW * RLOC + block_index // N_PROW * NB + global_row % NB

def reference(matrix, pivots):

    def apply_swap(column, anchor):
        target = pivots[column]
        at_column = anchor[column]
        at_target = anchor[target]
        return anchor.at[column].set(at_target).at[target].set(at_column)
    anchor = lax.fori_loop(0, NB, apply_swap, jnp.arange(NROWS, dtype=jnp.int32))
    every_row = jnp.arange(NROWS, dtype=jnp.int32)
    reorder = jnp.zeros((NROWS,), jnp.int32).at[storage(every_row)].set(storage(anchor))
    swapped = matrix[reorder]
    unit_lower = jnp.tril(matrix[:NB, :NB].astype(jnp.float32), -1) + jnp.eye(NB, dtype=jnp.float32)
    upper_rows = lax.linalg.triangular_solve(unit_lower, swapped[:NB, NB:].astype(jnp.float32), left_side=True, lower=True, unit_diagonal=True).astype(jnp.bfloat16)
    product = jnp.dot(matrix[NB:, :NB].astype(jnp.float32), upper_rows.astype(jnp.float32), preferred_element_type=jnp.float32)
    remainder = (swapped[NB:, NB:].astype(jnp.float32) - product).astype(jnp.bfloat16)
    top_part = jnp.concatenate([matrix[:NB, :NB], upper_rows], 1)
    bottom_part = jnp.concatenate([matrix[NB:, :NB], remainder], 1)
    return jnp.concatenate([top_part, bottom_part], 0)
```

```python
import functools

import jax
import jax.numpy as jnp
from jax import lax
from jax.experimental import pallas as pl
from jax.experimental.pallas import tpu as pltpu
from jax.sharding import PartitionSpec as P

NB = 256
HALF = 128
BF16 = jnp.bfloat16
F32 = jnp.float32
I32 = jnp.int32


def grid_of(row_groups):
    outer = 4 if row_groups % 4 == 0 else row_groups
    return outer, row_groups // outer


def round_rows(row_groups):
    share = -(-3 * NB // (2 * row_groups))
    return min(NB, -(-share // 16) * 16)


def iota(shape, dim):
    return lax.broadcasted_iota(I32, shape, dim)


def dot(a, b, precision=None):
    return jnp.dot(a, b, preferred_element_type=F32, precision=precision)


def block_owner(global_row, row_groups):
    block = lax.shift_right_logical(global_row, 8)
    if row_groups & (row_groups - 1) == 0:
        return block & (row_groups - 1), lax.shift_right_logical(block, row_groups.bit_length() - 1)
    return lax.rem(block, row_groups), lax.div(block, row_groups)


def plan_kernel(pivots, source, landing, anchor):
    def start(k, _):
        anchor[pivots[k]] = pivots[k]
        return 0

    def identity(k, _):
        anchor[k] = k
        return 0

    def swap(k, _):
        target = pivots[k]
        at_column, at_target = anchor[k], anchor[target]
        anchor[k] = at_target
        anchor[target] = at_column
        return 0

    def write(k, _):
        row = anchor[k]
        source[0, k] = row
        landing[0, k] = jnp.where(row >= NB, anchor[row], -1)
        return 0

    lax.fori_loop(0, NB, start, 0, unroll=8)
    lax.fori_loop(0, NB, identity, 0, unroll=8)
    lax.fori_loop(0, NB, swap, 0, unroll=8)
    lax.fori_loop(0, NB, write, 0, unroll=8)


def as_column(row):
    n = row.shape[1]
    wide = jnp.broadcast_to(row, (n, n))
    on_diagonal = iota((n, n), 0) == iota((n, n), 1)
    return jnp.sum(jnp.where(on_diagonal, wide, 0), axis=1, keepdims=True)


def pick_kernel(row_groups, cap, source, landing, matrix, rows, gather, place, flag, *gives):
    me = lax.axis_index("prow")
    outer, inner = grid_of(row_groups)
    src, land = source[...], landing[...]
    owner, block = block_owner(src, row_groups)
    local = block * NB + (src & (NB - 1))
    is_owner = (iota((row_groups, NB), 0) == owner).astype(BF16)
    upto = (iota((NB, NB), 0) <= iota((NB, NB), 1)).astype(BF16)
    ranks = dot(is_owner, upto)
    slot = jnp.sum(jnp.where(is_owner > 0, ranks, 0.0), axis=0, keepdims=True).astype(I32) - 1
    flag[...] = jnp.broadcast_to(jnp.max(ranks, axis=(0, 1), keepdims=True).astype(I32), flag.shape)
    code = jnp.where(slot < cap, owner * cap + slot, -1)

    def table(first, count, values):
        hit = code == iota((count, NB), 0) + first
        return jnp.max(jnp.where(hit, values, -1), axis=1, keepdims=True)

    my_rows = table(me * cap, cap, local)
    chosen = (my_rows == iota((cap, matrix.shape[0]), 1)).astype(BF16)
    rows[...] = dot(chosen, matrix[...]).astype(BF16)
    old_top = matrix[:NB]
    for j in range(inner):
        wanted = jnp.concatenate([table((z * inner + j) * cap, cap, land) for z in range(outer)], 0)
        chosen_top = (wanted == iota((outer * cap, NB), 1)).astype(BF16)
        gives[j][...] = dot(chosen_top, old_top).astype(BF16)
    code_column = as_column(code)
    lands_column = as_column(jnp.where(land >= 0, local, -1))
    mine = code_column - me * cap == iota((NB, HALF), 1)
    mine = mine & (iota((NB, HALF), 1) < cap)
    place[...] = jnp.max(jnp.where(mine, lands_column, -1), axis=0, keepdims=True)
    my_outer, my_inner = me // inner, me % inner
    for turn in range(inner):
        for step in range(outer):
            from_outer = lax.rem(my_outer - step + outer, outer)
            from_inner = lax.rem(my_inner - turn + inner, inner)
            first = (from_outer * inner + from_inner) * cap
            at = (turn * outer + step) * cap
            gather[:, at : at + cap] = (code_column == iota((NB, cap), 1) + first).astype(BF16)


def pieces(x):
    high = x.astype(BF16)
    rest = x - high.astype(F32)
    middle = rest.astype(BF16)
    return high, middle, (rest - middle.astype(F32)).astype(BF16)


def invert_kernel(block, inverse):
    rows, cols = iota((NB, NB), 0), iota((NB, NB), 1)
    lower = block[...].astype(F32)

    def corner(size):
        same = lax.div(rows, 2 * size) == lax.div(cols, 2 * size)
        low_left = ((rows & size) > 0) & ((cols & size) == 0)
        return jnp.where(same & low_left, lower, 0.0)

    x = jnp.where(rows == cols, 1.0, 0.0) - corner(1)
    size = 2
    while size < HALF:
        x = x - dot(x, dot(corner(size), x, lax.Precision.HIGHEST), lax.Precision.HIGHEST)
        size *= 2
    inverse[:HALF] = x[:HALF, :HALF]
    inverse[HALF:] = x[HALF:, HALF:]


def finish_kernel(row_groups, cap, *refs):
    outer, _ = grid_of(row_groups)
    matrix, block, inverse, panel, gather, place = refs[:6]
    parts = refs[6 : 6 + row_groups]
    arrived = refs[6 + row_groups : 6 + row_groups + outer]
    out, left, keep, first, corner, second = refs[6 + row_groups + outer :]
    tile = pl.program_id(0)
    row_me, col_me = lax.axis_index("prow"), lax.axis_index("pcol")
    height = matrix.shape[0]

    @pl.when(tile == 0)
    def _():
        hit = iota((height, HALF), 0) == place[...]
        kept = jnp.max(jnp.where(hit, 1.0, 0.0), axis=1, keepdims=True) == 0.0
        keep[...] = jnp.where(jnp.broadcast_to(kept, keep.shape), 1.0, 0.0)
        left[:, :NB] = -panel[...]
        left[:, NB:] = hit[:, :cap].astype(BF16)
        x1 = pieces(inverse[:HALF])
        x2 = pieces(inverse[HALF:])
        first[...] = jnp.concatenate(x1, 1)
        second[...] = jnp.concatenate([x2[0], x2[0], x2[1], x2[1], x2[0], x2[2]], 1)
        edge = block[HALF:, :HALF]
        corner[...] = jnp.concatenate([edge, edge, edge], 1)

        @pl.when(row_me == 0)
        def _():
            keep[:NB] = jnp.zeros((NB, HALF), F32)
            left[:NB, :NB] = (iota((NB, NB), 0) == iota((NB, NB), 1)).astype(BF16)
            left[:NB, NB:] = jnp.zeros((NB, cap), BF16)

    is_panel = (tile == 0) & (col_me == 0)

    @pl.when(is_panel)
    def _():
        out[...] = matrix[...]

    @pl.when(jnp.logical_not(is_panel))
    def _():
        rows = jnp.concatenate([part[...] for part in parts], 0)
        top = dot(gather[...], rows)
        top1 = top[:HALF].astype(BF16)
        upper1 = dot(first[...], jnp.concatenate([top1] * 3, 0))
        rest = top[HALF:] - dot(corner[...], jnp.concatenate(pieces(upper1), 0))
        high, middle, low = pieces(rest)
        upper2 = dot(second[...], jnp.concatenate([high, middle, high, middle, low, high], 0))
        swaps = jnp.where(row_me < row_groups // outer, arrived[0][...], jnp.zeros_like(arrived[0]))
        for other in arrived[1:]:
            swaps = swaps + other[...]
        right = jnp.concatenate([upper1.astype(BF16), upper2.astype(BF16), swaps], 0)
        change = dot(left[...], right)
        kept = jnp.concatenate([keep[...], keep[...]], 1) > 0.0
        out[...] = (jnp.where(kept, matrix[...].astype(F32), 0.0) + change).astype(BF16)


def spread(value, axes, index, pairs_of_levels):
    for pairs in pairs_of_levels:
        received = lax.ppermute(value, axes, pairs)
        takers = jnp.asarray([to for _, to in pairs], I32)
        value = jnp.where(jnp.any(index == takers), received, value)
    return value


def tree(count, stride=1):
    step, levels = count // 2, []
    while step:
        levels.append([(i * stride, (i + step) * stride) for i in range(0, count, 2 * step)])
        step //= 2
    return levels


def vmem(limit):
    return pltpu.CompilerParams(vmem_limit_bytes=limit)


def exchange(matrix, pivots):
    height, width = matrix.shape
    row_groups, col_groups = lax.axis_size("prow"), lax.axis_size("pcol")
    row_me, col_me = lax.axis_index("prow"), lax.axis_index("pcol")
    outer, inner = grid_of(row_groups)
    cap = round_rows(row_groups)
    shape = jax.ShapeDtypeStruct
    smem = pl.BlockSpec(memory_space=pltpu.SMEM)

    panel = spread(matrix[:, :NB], "pcol", col_me, tree(col_groups))
    both = ("prow", "pcol")
    me = row_me * col_groups + col_me
    block = spread(matrix[:NB, :NB], both, me, tree(row_groups, col_groups))
    block = spread(block, "pcol", col_me, tree(col_groups))

    source, landing = pl.pallas_call(
        plan_kernel,
        out_shape=[shape((1, NB), I32)] * 2,
        in_specs=[smem],
        out_specs=[smem, smem],
        scratch_shapes=[pltpu.SMEM((height * row_groups,), I32)],
        name="plan",
    )(pivots)

    whole = pl.BlockSpec(memory_space=pltpu.VMEM)
    rows, gather, place, flag, *gives = pl.pallas_call(
        functools.partial(pick_kernel, row_groups, cap),
        out_shape=[
            shape((cap, width), BF16),
            shape((NB, row_groups * cap), BF16),
            shape((1, HALF), I32),
            shape((1, HALF), I32),
        ]
        + [shape((outer * cap, width), BF16)] * inner,
        in_specs=[whole] * 3,
        out_specs=[whole] * (4 + inner),
        compiler_params=vmem(40 << 20),
        name="pick",
    )(source, landing, matrix)

    def at(o, i):
        return o % outer * inner + i % inner

    everyone = [(o, i) for o in range(outer) for i in range(inner)]
    parts = [rows]
    for step in range(1, outer):
        parts.append(lax.ppermute(rows, "prow", [(at(o, i), at(o + step, i)) for o, i in everyone]))
    for turn in range(1, inner):
        pairs = [(at(o, i), at(o, i + turn)) for o, i in everyone]
        parts += [lax.ppermute(part, "prow", pairs) for part in parts[:outer]]

    held = gives[0]
    for j in range(1, inner):
        held = jnp.where(row_me == j, lax.ppermute(gives[j], "prow", [(0, j)]), held)
    arrived = [held[:cap]]
    for step in range(1, outer):
        piece = held[step * cap : (step + 1) * cap]
        arrived.append(lax.ppermute(piece, "prow", [(i, at(step, i)) for i in range(inner)]))

    inverse = pl.pallas_call(
        invert_kernel,
        out_shape=shape((NB, HALF), F32),
        in_specs=[whole],
        out_specs=whole,
        name="invert",
    )(block)

    def full(x):
        return pl.BlockSpec(x.shape, lambda j: (0, 0))

    def columns(x):
        return pl.BlockSpec((x.shape[0], NB), lambda j: (0, j))

    result = pl.pallas_call(
        functools.partial(finish_kernel, row_groups, cap),
        out_shape=shape(matrix.shape, BF16),
        grid=(width // NB,),
        in_specs=[columns(matrix)]
        + [full(x) for x in (block, inverse, panel, gather, place)]
        + [columns(x) for x in (*parts, *arrived)],
        out_specs=columns(matrix),
        scratch_shapes=[
            pltpu.VMEM((height, NB + cap), BF16),
            pltpu.VMEM((height, HALF), F32),
            pltpu.VMEM((HALF, 3 * HALF), BF16),
            pltpu.VMEM((HALF, 3 * HALF), BF16),
            pltpu.VMEM((HALF, 6 * HALF), BF16),
        ],
        compiler_params=vmem(40 << 20),
        name="finish",
    )(matrix, block, inverse, panel, gather, place, *parts, *arrived)
    return result, flag[0, 0] > cap


def broadcast(block, axis, owner):
    block = jnp.where(lax.axis_index(axis) == owner, block, jnp.zeros_like(block))
    return lax.psum(block, axis)


def storage_row(global_row, rows_local, row_groups):
    block_index = global_row // NB
    return block_index % row_groups * rows_local + block_index // row_groups * NB + global_row % NB


def latest_match(targets, pivots, bound):
    steps = jnp.arange(NB, dtype=jnp.int32)
    hits = (pivots[None, :] == targets[:, None]) & (steps[None, :] < bound[:, None])
    return jnp.max(jnp.where(hits, steps[None, :], -1), axis=1)


def swap_anchor(pivots, wanted_rows):
    steps = jnp.arange(NB, dtype=jnp.int32)
    before = latest_match(steps, pivots, steps)
    pointer = jnp.where(before >= 0, before, steps)
    for level in range(NB.bit_length()):
        pointer = pointer[pointer]
    earlier = latest_match(pivots, pivots, steps)
    top_anchor = jnp.where(earlier >= 0, pointer[jnp.clip(earlier, 0, NB - 1)], pivots)
    last_hit = latest_match(wanted_rows, pivots, jnp.full(wanted_rows.shape, NB, jnp.int32))
    lower_anchor = jnp.where(last_hit >= 0, pointer[jnp.clip(last_hit, 0, NB - 1)], wanted_rows)
    in_top = wanted_rows < NB
    wanted_anchor = jnp.where(in_top, top_anchor[jnp.clip(wanted_rows, 0, NB - 1)], lower_anchor)
    return (top_anchor, wanted_anchor)


def general(matrix, pivots):
    rows_local, cols_local = matrix.shape
    row_groups = lax.axis_size("prow")
    prow_index = lax.axis_index("prow")
    pcol_index = lax.axis_index("pcol")
    local_rows = jnp.arange(rows_local, dtype=jnp.int32)
    global_rows = (local_rows // NB * row_groups + prow_index) * NB + local_rows % NB
    top_anchor, sources = swap_anchor(pivots, global_rows)
    top_sources = storage_row(top_anchor, rows_local, row_groups)
    owners = top_sources // rows_local
    nothing = jnp.zeros((), jnp.bfloat16)
    picked = jnp.where((owners == prow_index)[:, None], matrix[top_sources % rows_local], nothing)
    new_top = lax.psum(picked.astype(jnp.float32).astype(jnp.bfloat16), "prow")
    old_top = broadcast(matrix[:NB], "prow", 0)
    is_moved = (sources != global_rows) & (global_rows >= NB)
    displaced = old_top[jnp.clip(sources, 0, NB - 1)]
    exchanged = jnp.where(is_moved[:, None], displaced, matrix)
    panel = broadcast(matrix[:, :NB], "pcol", 0)
    diagonal_block = broadcast(panel[:NB], "prow", 0)
    unit_lower = jnp.tril(diagonal_block.astype(jnp.float32), -1) + jnp.eye(NB, dtype=jnp.float32)
    upper_rows = lax.linalg.triangular_solve(
        unit_lower, new_top.astype(jnp.float32), left_side=True, lower=True, unit_diagonal=True
    ).astype(jnp.bfloat16)
    is_top = global_rows < NB
    multipliers = jnp.where(is_top[:, None], nothing, panel)
    product = jnp.dot(multipliers, upper_rows, preferred_element_type=jnp.float32)
    updated = (exchanged.astype(jnp.float32) - product).astype(jnp.bfloat16)
    with_top = jnp.concatenate([upper_rows, updated[NB:]], 0)
    result = jnp.where(is_top[:, None], with_top, updated)
    panel_column = (pcol_index == 0) & (jnp.arange(cols_local) < NB)
    return jnp.where(panel_column[None, :], matrix, result)


def local(matrix, pivots):
    result, too_many = exchange(matrix, pivots)

    def again(state):
        return jnp.zeros((), jnp.bool_), general(matrix, pivots)

    return lax.while_loop(lambda state: state[0], again, (too_many, result))[1]


def solution(mesh):
    placed = (P("prow", "pcol"), P())
    return jax.shard_map(
        local, mesh=mesh, in_specs=placed, out_specs=P("prow", "pcol"), check_vma=False
    )
```

```python
import functools

import jax
import jax.numpy as jnp
from jax import lax
from jax.experimental import pallas as pl
from jax.experimental.pallas import tpu as pltpu
from jax.sharding import PartitionSpec as P

NB = 256
HALF = 128
BF16 = jnp.bfloat16
F32 = jnp.float32
I32 = jnp.int32


def grid_of(row_groups):
    outer = 4 if row_groups % 4 == 0 else row_groups
    return outer, row_groups // outer


def round_rows(row_groups):
    share = -(-3 * NB // (2 * row_groups))
    return min(NB, -(-share // 16) * 16)


def iota(shape, dim):
    return lax.broadcasted_iota(I32, shape, dim)


def dot(a, b):
    return jnp.dot(a, b, preferred_element_type=F32)


def block_owner(global_row, row_groups):
    block = lax.shift_right_logical(global_row, 8)
    if row_groups & (row_groups - 1) == 0:
        return block & (row_groups - 1), lax.shift_right_logical(block, row_groups.bit_length() - 1)
    return lax.rem(block, row_groups), lax.div(block, row_groups)


def place_of(source, row_groups):
    owner, block = block_owner(source, row_groups)
    return owner, block * NB + (source & (NB - 1))


def follow_swaps(pivots, anchor, source, landing):
    def start(k, _):
        anchor[pivots[k]] = pivots[k]
        return 0

    def swap(k, _):
        target = pivots[k]
        at_column, at_target = anchor[k], anchor[target]
        anchor[k] = at_target
        anchor[target] = at_column
        return 0

    def write(k, _):
        row = anchor[k]
        source[0, k] = row
        landing[0, k] = jnp.where(row >= NB, anchor[row], -1)
        return 0

    lax.fori_loop(0, NB, start, 0, unroll=16)
    for k in range(NB):
        anchor[k] = k
    lax.fori_loop(0, NB, swap, 0, unroll=16)
    lax.fori_loop(0, NB, write, 0, unroll=16)


def as_column(row):
    n = row.shape[1]
    wide = jnp.broadcast_to(row, (n, n))
    on_diagonal = iota((n, n), 0) == iota((n, n), 1)
    return jnp.sum(jnp.where(on_diagonal, wide, 0), axis=1, keepdims=True)


def pick_kernel(row_groups, cap, pivots, matrix, rows, source_out, landing_out, *scratch):
    held, anchor, source, landing, source_sem, landing_sem, sems = scratch
    height = matrix.shape[0]
    loads = []
    for i in range(height // NB):
        part = pl.ds(i * NB, NB)
        loads.append(pltpu.make_async_copy(matrix.at[part], held.at[part], sems.at[i]))
        loads[-1].start()
    follow_swaps(pivots, anchor, source, landing)
    one = pltpu.make_async_copy(source, source_out, source_sem)
    two = pltpu.make_async_copy(landing, landing_out, landing_sem)
    one.start()
    two.start()
    one.wait()
    two.wait()
    me = lax.axis_index("prow")
    owner, local = place_of(source_out[...], row_groups)
    slot, _ = slots_of(owner, row_groups)
    hit = (slot == iota((cap, NB), 0)) & (owner == me)
    my_rows = jnp.max(jnp.where(hit, local, -1), axis=1, keepdims=True)
    for load in loads:
        load.wait()
    chosen = (my_rows == iota((cap, height), 1)).astype(BF16)
    rows[...] = dot(chosen, held[...]).astype(BF16)


def slots_of(owner, row_groups):
    is_owner = (iota((row_groups, NB), 0) == owner).astype(BF16)
    upto = (iota((NB, NB), 0) <= iota((NB, NB), 1)).astype(BF16)
    ranks = dot(is_owner, upto)
    slot = jnp.sum(jnp.where(is_owner > 0, ranks, 0.0), axis=0, keepdims=True).astype(I32) - 1
    return slot, jnp.max(ranks, axis=(0, 1), keepdims=True).astype(I32)


def tables_kernel(row_groups, cap, source, landing, old_top, gather, place, flag, *gives):
    outer, inner = grid_of(row_groups)
    me = lax.axis_index("prow")
    land = landing[...]
    owner, local = place_of(source[...], row_groups)
    slot, most = slots_of(owner, row_groups)
    flag[...] = jnp.broadcast_to(most, flag.shape)
    code = jnp.where(slot < cap, owner * cap + slot, -1)
    for j in range(inner):
        wanted = []
        for z in range(outer):
            hit = code == iota((cap, NB), 0) + (z * inner + j) * cap
            wanted.append(jnp.max(jnp.where(hit, land, -1), axis=1, keepdims=True))
        chosen_top = (jnp.concatenate(wanted, 0) == iota((outer * cap, NB), 1)).astype(BF16)
        gives[j][...] = dot(chosen_top, old_top[...]).astype(BF16)
    code_column = as_column(code)
    lands_column = as_column(jnp.where(land >= 0, local, -1))
    mine = code_column - me * cap == iota((NB, HALF), 1)
    mine = mine & (iota((NB, HALF), 1) < cap)
    place[...] = jnp.max(jnp.where(mine, lands_column, -1), axis=0, keepdims=True)
    my_outer, my_inner = me // inner, me % inner
    for turn in range(inner):
        for step in range(outer):
            from_outer = lax.rem(my_outer - step + outer, outer)
            from_inner = lax.rem(my_inner - turn + inner, inner)
            first = (from_outer * inner + from_inner) * cap
            at = (turn * outer + step) * cap
            gather[:, at : at + cap] = (code_column == iota((NB, cap), 1) + first).astype(BF16)


def pick_all_kernel(row_groups, source, landing, matrix, rows, place):
    owner, local = place_of(source[...], row_groups)
    mine = owner == lax.axis_index("prow")
    wanted = as_column(jnp.where(mine, local, -1))
    chosen = (wanted == iota((NB, matrix.shape[0]), 1)).astype(BF16)
    rows[...] = dot(chosen, matrix[...]).astype(BF16)
    from_top = as_column(jnp.where(mine, landing[...], -1)) == iota((NB, NB), 1)
    place[...] = jnp.max(jnp.where(from_top, wanted, -1), axis=0, keepdims=True)


def pieces(x):
    high = x.astype(BF16)
    rest = x - high.astype(F32)
    middle = rest.astype(BF16)
    return high, middle, (rest - middle.astype(F32)).astype(BF16)


def invert_kernel(block, inverse):
    rows, cols = iota((NB, NB), 0), iota((NB, NB), 1)
    apart = rows ^ cols
    lower = jnp.where(rows > cols, block[...], jnp.zeros((), BF16))

    def corner(size):
        return jnp.where((apart >= size) & (apart < 2 * size), lower, jnp.zeros((), BF16))

    x = jnp.where(rows == cols, 1.0, 0.0) - corner(1).astype(F32)
    size = 2
    while size < HALF:
        high, middle, low = pieces(x)
        edge = corner(size)
        inner = (dot(edge, low) + dot(edge, middle)) + dot(edge, high)
        first, second, third = pieces(inner)
        small = (dot(high, third) + dot(low, first)) + dot(middle, second)
        x = x - ((small + (dot(high, second) + dot(middle, first))) + dot(high, first))
        size *= 2
    inverse[:HALF] = x[:HALF, :HALF]
    inverse[HALF:] = x[HALF:, HALF:]


def prepare_kernel(swaps, mine, received, place, left, keep):
    row_me, col_me = lax.axis_index("prow"), lax.axis_index("pcol")
    height = left.shape[0]

    @pl.when(col_me % 2 == 0)
    def _():
        left[:, :NB] = -mine[:height]

    @pl.when(col_me % 2 == 1)
    def _():
        left[:, :NB] = -received[:height]

    hit = iota((height, place.shape[1]), 0) == place[...]
    left[:, NB:] = hit[:, :swaps].astype(BF16)
    kept = jnp.max(jnp.where(hit, 1.0, 0.0), axis=1, keepdims=True) == 0.0
    keep[...] = jnp.where(jnp.broadcast_to(kept, keep.shape), 1.0, 0.0).astype(BF16)

    @pl.when(row_me == 0)
    def _():
        keep[:NB] = jnp.zeros((NB, HALF), BF16)
        left[:NB, :NB] = (iota((NB, NB), 0) == iota((NB, NB), 1)).astype(BF16)
        left[:NB, NB:] = jnp.zeros((NB, swaps), BF16)


def solve_kernel(block, inverse, gather, *refs):
    parts, upper = refs[:-1], refs[-1]
    rows = jnp.concatenate([part[...] for part in parts], 0)
    top = dot(gather[...], rows)
    top1 = top[:HALF].astype(BF16)
    first = jnp.concatenate(pieces(inverse[:HALF]), 1)
    upper1 = dot(first, jnp.concatenate([top1] * 3, 0))
    edge = block[HALF:, :HALF]
    edges = jnp.concatenate([edge, edge, edge], 1)
    rest = top[HALF:] - dot(edges, jnp.concatenate(pieces(upper1), 0))
    x, y, z = pieces(inverse[HALF:])
    high, middle, low = pieces(rest)
    second = jnp.concatenate([x, x, y, y, x, z], 1)
    upper[:HALF] = upper1.astype(BF16)
    upper[HALF:] = dot(second, jnp.concatenate([high, middle, high, middle, low, high], 0)).astype(BF16)


def update_kernel(matrix, left, keep, upper, *refs):
    arrived, (out, made, sems) = refs[:-3], refs[-3:]
    has_panel = lax.axis_index("pcol") == 0
    copies = []
    for j in range(matrix.shape[1] // NB):
        cols = slice(j * NB, (j + 1) * NB)

        def compute(cols=cols):
            swaps = arrived[0][:, cols]
            for other in arrived[1:]:
                swaps = swaps + other[:, cols]
            change = dot(left[...], jnp.concatenate([upper[:, cols], swaps], 0))
            kept = matrix[:, cols] * jnp.concatenate([keep[...], keep[...]], 1)
            made[:, cols] = (kept.astype(F32) + change).astype(BF16)

        def as_it_is(cols=cols):
            made[:, cols] = matrix[:, cols]

        if j == 0:
            pl.when(has_panel)(as_it_is)
            pl.when(jnp.logical_not(has_panel))(compute)
        else:
            compute()
        copies.append(pltpu.make_async_copy(made.at[:, cols], out.at[:, cols], sems.at[j]))
        copies[-1].start()
    for copy in copies:
        copy.wait()


SHAPE = jax.ShapeDtypeStruct
WHOLE = pl.BlockSpec(memory_space=pltpu.VMEM)


def params(limit=16):
    return pltpu.CompilerParams(vmem_limit_bytes=limit << 20)


def cost(flops=0, nbytes=0):
    return pl.CostEstimate(flops=flops, bytes_accessed=nbytes, transcendentals=0)


def prepare(height, swaps, mine, received, place):
    return pl.pallas_call(
        functools.partial(prepare_kernel, swaps),
        out_shape=[SHAPE((height, NB + swaps), BF16), SHAPE((height, HALF), BF16)],
        in_specs=[WHOLE] * 3,
        out_specs=[WHOLE] * 2,
        compiler_params=params(),
        name="prepare",
    )(mine, received, place)


def solve(width, block, inverse, gather, parts):
    return pl.pallas_call(
        solve_kernel,
        out_shape=SHAPE((NB, width), BF16),
        in_specs=[WHOLE] * (3 + len(parts)),
        out_specs=WHOLE,
        compiler_params=params(),
        name="solve",
    )(block, inverse, gather, *parts)


def update(matrix, left, keep, upper, arrived):
    return pl.pallas_call(
        update_kernel,
        out_shape=SHAPE(matrix.shape, BF16),
        in_specs=[WHOLE] * (4 + len(arrived)),
        out_specs=pl.BlockSpec(memory_space=pl.ANY),
        scratch_shapes=[
            pltpu.VMEM(matrix.shape, BF16),
            pltpu.SemaphoreType.DMA((matrix.shape[1] // NB,)),
        ],
        compiler_params=params(24),
        name="update",
    )(matrix, left, keep, upper, *arrived)


def spread(value, axes, index, count, stride=1, after_first=None):
    step = count // 2
    while step:
        pairs = [(i * stride, (i + step) * stride) for i in range(0, count, 2 * step)]
        received = lax.ppermute(value, axes, pairs)
        if after_first is not None and step == count // 2:
            received, after_first = lax.optimization_barrier((received, after_first))
        takes = lax.rem(index, 2 * step * stride) == step * stride
        value = jnp.where(takes, received, value)
        step //= 2
    return value if after_first is None else (value, *after_first)


def local(matrix, pivots):
    height, width = matrix.shape
    row_groups, col_groups = lax.axis_size("prow"), lax.axis_size("pcol")
    row_me, col_me = lax.axis_index("prow"), lax.axis_index("pcol")
    outer, inner = grid_of(row_groups)
    cap = round_rows(row_groups)
    smem = pl.BlockSpec(memory_space=pltpu.SMEM)

    rows, source, landing = pl.pallas_call(
        functools.partial(pick_kernel, row_groups, cap),
        out_shape=[SHAPE((cap, width), BF16), SHAPE((1, NB), I32), SHAPE((1, NB), I32)],
        in_specs=[smem, pl.BlockSpec(memory_space=pl.ANY)],
        out_specs=[WHOLE] * 3,
        scratch_shapes=[
            pltpu.VMEM((height, width), BF16),
            pltpu.SMEM((height * row_groups,), I32),
            pltpu.SMEM((1, NB), I32),
            pltpu.SMEM((1, NB), I32),
            pltpu.SemaphoreType.DMA,
            pltpu.SemaphoreType.DMA,
            pltpu.SemaphoreType.DMA((height // NB,)),
        ],
        compiler_params=params(12),
        cost_estimate=cost(2 * 4 * cap * width * height, 20 << 20),
        name="pick",
    )(pivots, matrix)
    gather, place, flag, *gives = pl.pallas_call(
        functools.partial(tables_kernel, row_groups, cap),
        out_shape=[SHAPE((NB, row_groups * cap), BF16), SHAPE((1, HALF), I32), SHAPE((1, HALF), I32)]
        + [SHAPE((outer * cap, width), BF16)] * inner,
        grid=(1,),
        in_specs=[pl.BlockSpec((1, NB), lambda i: (0, 0))] * 2 + [pl.BlockSpec((NB, width), lambda i: (0, 0))],
        out_specs=[WHOLE] * (3 + inner),
        compiler_params=params(12),
        cost_estimate=cost(2 * 4 * cap * width * height, 4 << 20),
        name="tables",
    )(source, landing, matrix)

    both = ("prow", "pcol")
    me = row_me * col_groups + col_me
    block, flag = spread(matrix[:NB, :NB], both, me, row_groups, col_groups, (flag,))
    block = spread(block, "pcol", col_me, col_groups)
    panel = matrix[:, :NB]
    step = col_groups // 2
    while step > 1:
        pairs = [(i, i + step) for i in range(0, col_groups, 2 * step)]
        received = lax.ppermute(panel, "pcol", pairs)
        panel = jnp.where(lax.rem(col_me, 2 * step) == step, received, panel)
        step //= 2
    passed = lax.ppermute(panel, "pcol", [(i, i + 1) for i in range(0, col_groups, 2)])

    def at(o, i):
        return o % outer * inner + i % inner

    everyone = [(o, i) for o in range(outer) for i in range(inner)]
    parts = [rows]
    for step in range(1, outer):
        parts.append(lax.ppermute(rows, "prow", [(at(o, i), at(o + step, i)) for o, i in everyone]))
    parts = [jnp.concatenate(parts, 0)]
    for turn in range(1, inner):
        parts.append(lax.ppermute(parts[0], "prow", [(at(o, i), at(o, i + turn)) for o, i in everyone]))

    held = gives[0]
    for j in range(1, inner):
        held = jnp.where(row_me == j, lax.ppermute(gives[j], "prow", [(0, j)]), held)
    arrived = [jnp.where(row_me < inner, held[:cap], jnp.zeros((), BF16))]
    for step in range(1, outer):
        piece = held[step * cap : (step + 1) * cap]
        arrived.append(lax.ppermute(piece, "prow", [(i, at(step, i)) for i in range(inner)]))

    inverse = pl.pallas_call(
        invert_kernel,
        out_shape=SHAPE((NB, HALF), F32),
        in_specs=[WHOLE],
        out_specs=WHOLE,
        cost_estimate=cost(2 * 60 * NB * NB * NB),
        name="invert",
    )(block)

    left, keep = prepare(height, cap, panel, passed, place)
    upper = solve(width, block, inverse, gather, parts)
    result = update(matrix, left, keep, upper, arrived)

    def again(state):
        picked, place_all = pl.pallas_call(
            functools.partial(pick_all_kernel, row_groups),
            out_shape=[SHAPE((NB, width), BF16), SHAPE((1, NB), I32)],
            in_specs=[WHOLE] * 3,
            out_specs=[WHOLE] * 2,
            compiler_params=params(),
            name="pick_all",
        )(source, landing, matrix)
        top = picked
        for shift in range(1, row_groups):
            top = top + lax.ppermute(picked, "prow", [(i, (i + shift) % row_groups) for i in range(row_groups)])
        same = (iota((NB, NB), 0) == iota((NB, NB), 1)).astype(BF16)
        old_top = spread(matrix[:NB], "prow", row_me, row_groups)
        left_all, keep_all = prepare(height, NB, panel, passed, place_all)
        upper_all = solve(width, block, inverse, same, [top])
        return jnp.zeros((), jnp.bool_), update(matrix, left_all, keep_all, upper_all, [old_top])

    return lax.while_loop(lambda state: state[0], again, (flag[0, 0] > cap, result))[1]


def solution(mesh):
    placed = (P("prow", "pcol"), P())
    return jax.shard_map(
        local, mesh=mesh, in_specs=placed, out_specs=P("prow", "pcol"), check_vma=False
    )
```

```python
import functools

import jax
import jax.numpy as jnp
from jax import lax
from jax.experimental import pallas as pl
from jax.experimental.pallas import tpu as pltpu
from jax.sharding import PartitionSpec as P

NB = 256
HALF = 128
BF16 = jnp.bfloat16
F32 = jnp.float32
I32 = jnp.int32


def grid_of(row_groups):
    outer = 4 if row_groups % 4 == 0 else row_groups
    return outer, row_groups // outer


def round_rows(row_groups):
    share = -(-3 * NB // (2 * row_groups))
    return min(NB, -(-share // 16) * 16)


def iota(shape, dim):
    return lax.broadcasted_iota(I32, shape, dim)


def dot(a, b):
    return jnp.dot(a, b, preferred_element_type=F32)


def block_owner(global_row, row_groups):
    block = lax.shift_right_logical(global_row, 8)
    if row_groups & (row_groups - 1) == 0:
        return block & (row_groups - 1), lax.shift_right_logical(block, row_groups.bit_length() - 1)
    return lax.rem(block, row_groups), lax.div(block, row_groups)


def place_of(source, row_groups):
    owner, block = block_owner(source, row_groups)
    return owner, block * NB + (source & (NB - 1))


def follow_swaps(pivots, anchor, source, landing, source_out, landing_out, source_sem, landing_sem):
    def start(k, _):
        anchor[pivots[k]] = pivots[k]
        return 0

    def swap(k, _):
        target = pivots[k]
        at_column, at_target = anchor[k], anchor[target]
        anchor[k] = at_target
        anchor[target] = at_column
        return 0

    def write(k, _):
        row = anchor[k]
        source[0, k] = row
        landing[0, k] = jnp.where(row >= NB, anchor[row], -1)
        return 0

    lax.fori_loop(0, NB, start, 0, unroll=16)
    for k in range(NB):
        anchor[k] = k
    lax.fori_loop(0, NB, swap, 0, unroll=16)
    lax.fori_loop(0, NB, write, 0, unroll=16)
    one = pltpu.make_async_copy(source, source_out, source_sem)
    two = pltpu.make_async_copy(landing, landing_out, landing_sem)
    one.start()
    two.start()
    one.wait()
    two.wait()


def as_column(row):
    n = row.shape[1]
    wide = jnp.broadcast_to(row, (n, n))
    on_diagonal = iota((n, n), 0) == iota((n, n), 1)
    return jnp.sum(jnp.where(on_diagonal, wide, 0), axis=1, keepdims=True)


def pick_kernel(row_groups, cap, pivots, matrix, rows, source_out, landing_out, *refs):
    outer, inner = grid_of(row_groups)
    gives, scratch = refs[:inner], refs[inner:]
    held, anchor, source, landing, source_sem, landing_sem, sems = scratch
    height = matrix.shape[0]
    loads = []
    for i in range(height // NB):
        part = pl.ds(i * NB, NB)
        loads.append(pltpu.make_async_copy(matrix.at[part], held.at[part], sems.at[i]))
        loads[-1].start()
    follow_swaps(pivots, anchor, source, landing, source_out, landing_out, source_sem, landing_sem)
    me = lax.axis_index("prow")
    owner, local = place_of(source_out[...], row_groups)
    slot, _ = slots_of(owner, row_groups)
    hit = (slot == iota((cap, NB), 0)) & (owner == me)
    my_rows = jnp.max(jnp.where(hit, local, -1), axis=1, keepdims=True)
    for load in loads:
        load.wait()
    chosen = (my_rows == iota((cap, height), 1)).astype(BF16)
    rows[...] = dot(chosen, held[...]).astype(BF16)
    land = landing_out[...]
    code = jnp.where(slot < cap, owner * cap + slot, -1)
    for j in range(inner):
        wanted = []
        for z in range(outer):
            hit = code == iota((cap, NB), 0) + (z * inner + j) * cap
            wanted.append(jnp.max(jnp.where(hit, land, -1), axis=1, keepdims=True))
        chosen_top = (jnp.concatenate(wanted, 0) == iota((outer * cap, NB), 1)).astype(BF16)
        gives[j][...] = dot(chosen_top, held[:NB]).astype(BF16)


def slots_of(owner, row_groups):
    is_owner = (iota((row_groups, NB), 0) == owner).astype(BF16)
    upto = (iota((NB, NB), 0) <= iota((NB, NB), 1)).astype(BF16)
    ranks = dot(is_owner, upto)
    slot = jnp.sum(jnp.where(is_owner > 0, ranks, 0.0), axis=0, keepdims=True).astype(I32) - 1
    return slot, jnp.max(ranks, axis=(0, 1), keepdims=True).astype(I32)


def tables_kernel(row_groups, cap, source, landing, gather, place, flag):
    outer, inner = grid_of(row_groups)
    me = lax.axis_index("prow")
    land = landing[...]
    owner, local = place_of(source[...], row_groups)
    slot, most = slots_of(owner, row_groups)
    flag[...] = jnp.broadcast_to(most, flag.shape)
    code = jnp.where(slot < cap, owner * cap + slot, -1)
    code_column = as_column(code)
    lands_column = as_column(jnp.where(land >= 0, local, -1))
    mine = code_column - me * cap == iota((NB, HALF), 1)
    mine = mine & (iota((NB, HALF), 1) < cap)
    place[...] = jnp.max(jnp.where(mine, lands_column, -1), axis=0, keepdims=True)
    my_outer, my_inner = me // inner, me % inner
    for turn in range(inner):
        for step in range(outer):
            from_outer = lax.rem(my_outer - step + outer, outer)
            from_inner = lax.rem(my_inner - turn + inner, inner)
            first = (from_outer * inner + from_inner) * cap
            at = (turn * outer + step) * cap
            gather[:, at : at + cap] = (code_column == iota((NB, cap), 1) + first).astype(BF16)


def turn_kernel(row_groups, cap, *refs):
    outer, inner = grid_of(row_groups)
    parts, own, bundles = refs[:outer], refs[outer], refs[outer + 1 : outer + inner]
    gathered, *sent = refs[outer + inner :]
    me = lax.axis_index("prow")
    for i, part in enumerate(parts):
        gathered[i * cap : (i + 1) * cap] = part[...]

    def pass_on(bundle):
        for i, piece in enumerate(sent):
            piece[...] = bundle[i * cap : (i + 1) * cap]

    pl.when(me == 0)(lambda: pass_on(own))
    for j, bundle in enumerate(bundles):
        pl.when(me == j + 1)(functools.partial(pass_on, bundle))

    @pl.when(me >= inner)
    def _():
        for piece in sent:
            piece[...] = jnp.zeros(piece.shape, BF16)


def pick_all_kernel(row_groups, pivots, matrix, rows, place, *scratch):
    source, landing, anchor, source_in, landing_in, source_sem, landing_sem = scratch
    follow_swaps(pivots, anchor, source_in, landing_in, source, landing, source_sem, landing_sem)
    owner, local = place_of(source[...], row_groups)
    mine = owner == lax.axis_index("prow")
    wanted = as_column(jnp.where(mine, local, -1))
    chosen = (wanted == iota((NB, matrix.shape[0]), 1)).astype(BF16)
    rows[...] = dot(chosen, matrix[...]).astype(BF16)
    from_top = as_column(jnp.where(mine, landing[...], -1)) == iota((NB, NB), 1)
    place[...] = jnp.max(jnp.where(from_top, wanted, -1), axis=0, keepdims=True)


def pieces(x):
    high = x.astype(BF16)
    rest = x - high.astype(F32)
    middle = rest.astype(BF16)
    return high, middle, (rest - middle.astype(F32)).astype(BF16)


def invert_kernel(block, inverse):
    rows, cols = iota((HALF, HALF), 0), iota((HALF, HALF), 1)
    apart = rows ^ cols
    none = jnp.zeros((), BF16)
    halves = [slice(0, HALF), slice(HALF, NB)]
    lowers = [jnp.where(rows > cols, block[part, part], none) for part in halves]

    def corner(lower, size):
        return jnp.where((apart >= size) & (apart < 2 * size), lower, none)

    found = [jnp.where(rows == cols, 1.0, 0.0) - corner(lower, 1).astype(F32) for lower in lowers]
    size = 2
    while size < HALF:
        for i, lower in enumerate(lowers):
            x, edge = found[i], corner(lower, size)
            high, middle, low = pieces(x)
            first, second, third = pieces((dot(edge, low) + dot(edge, middle)) + dot(edge, high))
            small = (dot(high, third) + dot(low, first)) + dot(middle, second)
            found[i] = x - ((small + (dot(high, second) + dot(middle, first))) + dot(high, first))
        size *= 2
    for part, x in zip(halves, found):
        inverse[part] = x


def finish_kernel(n_parts, swaps, *refs):
    matrix, mine, passed, place, block, inverse, gather = refs[:7]
    parts, arrived = refs[7 : 7 + n_parts], refs[7 + n_parts : -7]
    out, made, left, keep, upper, load_sems, store_sems = refs[-7:]
    row_me, col_me = lax.axis_index("prow"), lax.axis_index("pcol")
    height, width = made.shape
    loads = []
    for i in range(height // NB):
        part = pl.ds(i * NB, NB)
        loads.append(pltpu.make_async_copy(matrix.at[part], made.at[part], load_sems.at[i]))
        loads[-1].start()

    @pl.when(col_me % 2 == 0)
    def _():
        left[:, :NB] = -mine[:height]

    @pl.when(col_me % 2 == 1)
    def _():
        left[:, :NB] = -passed[:height]

    hit = (iota((height, place.shape[1]), 0) == place[...]).astype(BF16)
    left[:, NB:] = hit[:, :swaps]
    gone = dot(hit, jnp.ones((place.shape[1], HALF), BF16))
    keep[...] = (1.0 - gone).astype(BF16)

    @pl.when(row_me == 0)
    def _():
        keep[:NB] = jnp.zeros((NB, HALF), BF16)
        left[:NB, :NB] = (iota((NB, NB), 0) == iota((NB, NB), 1)).astype(BF16)
        left[:NB, NB:] = jnp.zeros((NB, swaps), BF16)

    rows = jnp.concatenate([part[...] for part in parts], 0)
    top = dot(gather[...], rows)
    top1 = top[:HALF].astype(BF16)
    first = jnp.concatenate(pieces(inverse[:HALF]), 1)
    upper1 = dot(first, jnp.concatenate([top1] * 3, 0))
    edge = block[HALF:, :HALF]
    edges = jnp.concatenate([edge, edge, edge], 1)
    rest = top[HALF:] - dot(edges, jnp.concatenate(pieces(upper1), 0))
    x, y, z = pieces(inverse[HALF:])
    high, middle, low = pieces(rest)
    second = jnp.concatenate([x, x, y, y, x, z], 1)
    upper[:HALF] = upper1.astype(BF16)
    upper[HALF:NB] = dot(second, jnp.concatenate([high, middle, high, middle, low, high], 0)).astype(BF16)
    moved = arrived[0][...]
    for other in arrived[1:]:
        moved = moved + other[...]
    upper[NB:] = moved

    for load in loads:
        load.wait()
    stores = []
    for j in range(width // NB):
        cols = slice(j * NB, (j + 1) * NB)

        def compute(cols=cols):
            change = dot(left[...], upper[:, cols])
            kept = made[:, cols] * jnp.concatenate([keep[...], keep[...]], 1)
            made[:, cols] = (kept.astype(F32) + change).astype(BF16)

        if j == 0:
            pl.when(col_me != 0)(compute)
        else:
            compute()
        stores.append(pltpu.make_async_copy(made.at[:, cols], out.at[:, cols], store_sems.at[j]))
        stores[-1].start()
    for store in stores:
        store.wait()


SHAPE = jax.ShapeDtypeStruct
WHOLE = pl.BlockSpec(memory_space=pltpu.VMEM)


def params(limit=16):
    return pltpu.CompilerParams(vmem_limit_bytes=limit << 20)


def cost(flops=0, nbytes=0):
    return pl.CostEstimate(flops=flops, bytes_accessed=nbytes, transcendentals=0)


def finish(matrix, panel, passed, place, block, inverse, gather, parts, arrived):
    height, width = matrix.shape
    swaps = arrived[0].shape[0]
    return pl.pallas_call(
        functools.partial(finish_kernel, len(parts), swaps),
        out_shape=SHAPE(matrix.shape, BF16),
        in_specs=[pl.BlockSpec(memory_space=pl.ANY)] + [WHOLE] * (6 + len(parts) + len(arrived)),
        out_specs=pl.BlockSpec(memory_space=pl.ANY),
        scratch_shapes=[
            pltpu.VMEM((height, width), BF16),
            pltpu.VMEM((height, NB + swaps), BF16),
            pltpu.VMEM((height, HALF), BF16),
            pltpu.VMEM((NB + swaps, width), BF16),
            pltpu.SemaphoreType.DMA((height // NB,)),
            pltpu.SemaphoreType.DMA((width // NB,)),
        ],
        compiler_params=params(20),
        name="finish",
    )(matrix, panel, passed, place, block, inverse, gather, *parts, *arrived)


def spread(value, axes, index, count):
    step = count // 2
    while step:
        pairs = [(i, i + step) for i in range(0, count, 2 * step)]
        received = lax.ppermute(value, axes, pairs)
        value = jnp.where(lax.rem(index, 2 * step) == step, received, value)
        step //= 2
    return value


def two_rounds(row_groups):
    outer, inner = grid_of(row_groups)

    def hops(pair):
        a, b = pair
        return abs(a // inner - b // inner) + abs(a % inner - b % inner)

    count = 0
    while (count + 1) ** 2 < row_groups:
        count += 1
    holders = [0, outer // 2 * inner]
    holders += [i for i in range(row_groups) if i not in holders][: count - 1]
    left = [i for i in range(row_groups) if i not in holders]
    second = []
    while left:
        pairs, free = [], list(holders)
        while free and left:
            best = min(((a, b) for a in free for b in left), key=hops)
            pairs.append(best)
            free.remove(best[0])
            left.remove(best[1])
        second.append(pairs)
    return [[(0, i)] for i in holders[1:]], second


def local(matrix, pivots):
    height, width = matrix.shape
    row_groups, col_groups = lax.axis_size("prow"), lax.axis_size("pcol")
    row_me, col_me = lax.axis_index("prow"), lax.axis_index("pcol")
    outer, inner = grid_of(row_groups)
    cap = round_rows(row_groups)
    smem = pl.BlockSpec(memory_space=pltpu.SMEM)

    rows_out = [SHAPE((1, NB), I32), SHAPE((1, NB), I32)]
    swap_scratch = [
        pltpu.SMEM((height * row_groups,), I32),
        pltpu.SMEM((1, NB), I32),
        pltpu.SMEM((1, NB), I32),
        pltpu.SemaphoreType.DMA,
        pltpu.SemaphoreType.DMA,
    ]
    rows, source, landing, *gives = pl.pallas_call(
        functools.partial(pick_kernel, row_groups, cap),
        out_shape=[SHAPE((cap, width), BF16)] + rows_out + [SHAPE((outer * cap, width), BF16)] * inner,
        in_specs=[smem, pl.BlockSpec(memory_space=pl.ANY)],
        out_specs=[WHOLE] * (3 + inner),
        scratch_shapes=[pltpu.VMEM((height, width), BF16)]
        + swap_scratch
        + [pltpu.SemaphoreType.DMA((height // NB,))],
        compiler_params=params(16),
        cost_estimate=cost(2 * 4 * cap * width * height, 20 << 20),
        name="pick",
    )(pivots, matrix)
    gather, place, flag = pl.pallas_call(
        functools.partial(tables_kernel, row_groups, cap),
        out_shape=[SHAPE((NB, row_groups * cap), BF16), SHAPE((1, HALF), I32), SHAPE((1, HALF), I32)],
        in_specs=[WHOLE] * 2,
        out_specs=[WHOLE] * 3,
        compiler_params=params(),
        cost_estimate=cost(1 << 35, 32 << 20),
        name="tables",
    )(source, landing)

    both = ("prow", "pcol")
    me = row_me * col_groups + col_me
    first_round, second_round = two_rounds(row_groups)

    def send(value, rounds):
        for pairs in rounds:
            yield pairs, lax.ppermute(value, both, [(a * col_groups, b * col_groups) for a, b in pairs])

    def take(value, received):
        for pairs, other in received:
            takes = functools.reduce(jnp.logical_or, [me == b * col_groups for _, b in pairs])
            value = jnp.where(takes, other, value)
        return value

    def at(o, i):
        return o % outer * inner + i % inner

    everyone = [(o, i) for o in range(outer) for i in range(inner)]

    block = matrix[:NB, :NB]
    received = list(send(block, first_round))

    parts = [rows]
    for step in range(1, outer):
        parts.append(lax.ppermute(rows, "prow", [(at(o, i), at(o + step, i)) for o, i in everyone]))
    bundles = [lax.ppermute(gives[j], "prow", [(0, j)]) for j in range(1, inner)]
    arrays, _ = lax.optimization_barrier(([other for _, other in received], place))
    block = take(block, [(pairs, other) for (pairs, _), other in zip(received, arrays)])
    block = take(block, list(send(block, second_round)))
    panel = jnp.concatenate([matrix[:, :NB], block], 0)
    half = col_groups // 2
    hop = lax.ppermute(panel, "pcol", [(0, half)])
    gathered, *sent = pl.pallas_call(
        functools.partial(turn_kernel, row_groups, cap),
        out_shape=[SHAPE((outer * cap, width), BF16)] + [SHAPE((cap, width), BF16)] * outer,
        in_specs=[WHOLE] * (outer + inner),
        out_specs=[WHOLE] * (1 + outer),
        compiler_params=params(8),
        name="turn",
    )(*parts, gives[0], *bundles)

    hop, sent = lax.optimization_barrier((hop, sent))
    panel = jnp.where(col_me == half, hop, panel)
    step = half // 2
    while step > 1:
        received = lax.ppermute(panel, "pcol", [(i, i + step) for i in range(0, col_groups, 2 * step)])
        panel = jnp.where(lax.rem(col_me, 2 * step) == step, received, panel)
        step //= 2

    parts = [gathered]
    for turn in range(1, inner):
        parts.append(lax.ppermute(gathered, "prow", [(at(o, i), at(o, i + turn)) for o, i in everyone]))
    arrived = [sent[0]]
    for step in range(1, outer):
        arrived.append(lax.ppermute(sent[step], "prow", [(i, at(step, i)) for i in range(inner)]))
    passed = lax.ppermute(panel, "pcol", [(i, i + 1) for i in range(0, col_groups, 2)])
    block = jnp.where(lax.rem(col_me, 2) == 1, passed[height:], panel[height:])
    inverse = pl.pallas_call(
        invert_kernel,
        out_shape=SHAPE((NB, HALF), F32),
        in_specs=[WHOLE],
        out_specs=WHOLE,
        cost_estimate=cost(2 * 60 * NB * NB * NB),
        name="invert",
    )(block)
    result = finish(matrix, panel, passed, place, block, inverse, gather, parts, arrived)

    def again(state):
        picked, place_all = pl.pallas_call(
            functools.partial(pick_all_kernel, row_groups),
            out_shape=[SHAPE((NB, width), BF16), SHAPE((1, NB), I32)],
            in_specs=[smem, WHOLE],
            out_specs=[WHOLE] * 2,
            scratch_shapes=[pltpu.VMEM((1, NB), I32)] * 2 + swap_scratch,
            compiler_params=params(),
            name="pick_all",
        )(pivots, matrix)
        top = picked
        for shift in range(1, row_groups):
            top = top + lax.ppermute(picked, "prow", [(i, (i + shift) % row_groups) for i in range(row_groups)])
        same = (iota((NB, NB), 0) == iota((NB, NB), 1)).astype(BF16)
        old_top = spread(matrix[:NB], "prow", row_me, row_groups)
        again_made = finish(matrix, panel, passed, place_all, block, inverse, same, [top], [old_top])
        return jnp.zeros((), jnp.bool_), again_made

    return lax.while_loop(lambda state: state[0], again, (flag[0, 0] > cap, result))[1]


def solution(mesh):
    placed = (P("prow", "pcol"), P())
    return jax.shard_map(
        local, mesh=mesh, in_specs=placed, out_specs=P("prow", "pcol"), check_vma=False
    )
```

```python
import functools

import jax
import jax.numpy as jnp
from jax import lax
from jax.experimental import pallas as pl
from jax.experimental.pallas import tpu as pltpu
from jax.sharding import PartitionSpec as P

NB = 256
HALF = 128
BF16 = jnp.bfloat16
F32 = jnp.float32
I32 = jnp.int32


def grid_of(row_groups):
    outer = 4 if row_groups % 4 == 0 else row_groups
    return outer, row_groups // outer


def round_rows(row_groups):
    share = -(-3 * NB // (2 * row_groups))
    return min(NB, -(-share // 16) * 16)


def iota(shape, dim):
    return lax.broadcasted_iota(I32, shape, dim)


def dot(a, b):
    return jnp.dot(a, b, preferred_element_type=F32)


def block_owner(global_row, row_groups):
    block = lax.shift_right_logical(global_row, 8)
    if row_groups & (row_groups - 1) == 0:
        return block & (row_groups - 1), lax.shift_right_logical(block, row_groups.bit_length() - 1)
    return lax.rem(block, row_groups), lax.div(block, row_groups)


def place_of(source, row_groups):
    owner, block = block_owner(source, row_groups)
    return owner, block * NB + (source & (NB - 1))


def follow_swaps(pivots, anchor, source, landing, source_out, landing_out, source_sem, landing_sem):
    def start(k, _):
        anchor[pivots[k]] = pivots[k]
        return 0

    def swap(k, _):
        target = pivots[k]
        at_column, at_target = anchor[k], anchor[target]
        anchor[k] = at_target
        anchor[target] = at_column
        return 0

    def write(k, _):
        row = anchor[k]
        source[0, k] = row
        landing[0, k] = jnp.where(row >= NB, anchor[row], -1)
        return 0

    lax.fori_loop(0, NB, start, 0, unroll=16)
    for k in range(NB):
        anchor[k] = k
    lax.fori_loop(0, NB, swap, 0, unroll=16)
    lax.fori_loop(0, NB, write, 0, unroll=16)
    one = pltpu.make_async_copy(source, source_out, source_sem)
    two = pltpu.make_async_copy(landing, landing_out, landing_sem)
    one.start()
    two.start()
    one.wait()
    two.wait()


def as_column(row):
    n = row.shape[1]
    wide = jnp.broadcast_to(row, (n, n))
    on_diagonal = iota((n, n), 0) == iota((n, n), 1)
    return jnp.sum(jnp.where(on_diagonal, wide, 0), axis=1, keepdims=True)


def pick_kernel(row_groups, cap, pivots, matrix, rows, source_out, landing_out, *refs):
    outer, inner = grid_of(row_groups)
    gives, scratch = refs[:inner], refs[inner:]
    held, anchor, source, landing, source_sem, landing_sem, sems = scratch
    height = matrix.shape[0]
    loads = []
    for i in range(height // NB):
        part = pl.ds(i * NB, NB)
        loads.append(pltpu.make_async_copy(matrix.at[part], held.at[part], sems.at[i]))
        loads[-1].start()
    follow_swaps(pivots, anchor, source, landing, source_out, landing_out, source_sem, landing_sem)
    me = lax.axis_index("prow")
    owner, local = place_of(source_out[...], row_groups)
    slot, _ = slots_of(owner, row_groups)
    hit = (slot == iota((cap, NB), 0)) & (owner == me)
    my_rows = jnp.max(jnp.where(hit, local, -1), axis=1, keepdims=True)
    for load in loads:
        load.wait()
    chosen = (my_rows == iota((cap, height), 1)).astype(BF16)
    rows[...] = dot(chosen, held[...]).astype(BF16)
    land = landing_out[...]
    code = jnp.where(slot < cap, owner * cap + slot, -1)
    for j in range(inner):
        wanted = []
        for z in range(outer):
            hit = code == iota((cap, NB), 0) + (z * inner + j) * cap
            wanted.append(jnp.max(jnp.where(hit, land, -1), axis=1, keepdims=True))
        chosen_top = (jnp.concatenate(wanted, 0) == iota((outer * cap, NB), 1)).astype(BF16)
        gives[j][...] = dot(chosen_top, held[:NB]).astype(BF16)


def slots_of(owner, row_groups):
    is_owner = (iota((row_groups, NB), 0) == owner).astype(BF16)
    upto = (iota((NB, NB), 0) <= iota((NB, NB), 1)).astype(BF16)
    ranks = dot(is_owner, upto)
    slot = jnp.sum(jnp.where(is_owner > 0, ranks, 0.0), axis=0, keepdims=True).astype(I32) - 1
    return slot, jnp.max(ranks, axis=(0, 1), keepdims=True).astype(I32)


def tables_kernel(row_groups, cap, source, landing, gather, place, flag):
    outer, inner = grid_of(row_groups)
    me = lax.axis_index("prow")
    land = landing[...]
    owner, local = place_of(source[...], row_groups)
    slot, most = slots_of(owner, row_groups)
    flag[...] = jnp.broadcast_to(most, flag.shape)
    code = jnp.where(slot < cap, owner * cap + slot, -1)
    code_column = as_column(code)
    lands_column = as_column(jnp.where(land >= 0, local, -1))
    mine = code_column - me * cap == iota((NB, HALF), 1)
    mine = mine & (iota((NB, HALF), 1) < cap)
    place[...] = jnp.max(jnp.where(mine, lands_column, -1), axis=0, keepdims=True)
    my_outer, my_inner = me // inner, me % inner
    for turn in range(inner):
        for step in range(outer):
            from_outer = lax.rem(my_outer - step + outer, outer)
            from_inner = lax.rem(my_inner - turn + inner, inner)
            first = (from_outer * inner + from_inner) * cap
            at = (turn * outer + step) * cap
            gather[:, at : at + cap] = (code_column == iota((NB, cap), 1) + first).astype(BF16)


def turn_kernel(row_groups, cap, *refs):
    outer, inner = grid_of(row_groups)
    parts, own, bundles = refs[:outer], refs[outer], refs[outer + 1 : outer + inner]
    gathered, *sent = refs[outer + inner :]
    me = lax.axis_index("prow")
    for i, part in enumerate(parts):
        gathered[i * cap : (i + 1) * cap] = part[...]

    def pass_on(bundle):
        for i, piece in enumerate(sent):
            piece[...] = bundle[i * cap : (i + 1) * cap]

    pl.when(me == 0)(lambda: pass_on(own))
    for j, bundle in enumerate(bundles):
        pl.when(me == j + 1)(functools.partial(pass_on, bundle))

    @pl.when(me >= inner)
    def _():
        for piece in sent:
            piece[...] = jnp.zeros(piece.shape, BF16)


def pick_all_kernel(row_groups, pivots, matrix, rows, place, *scratch):
    source, landing, anchor, source_in, landing_in, source_sem, landing_sem = scratch
    follow_swaps(pivots, anchor, source_in, landing_in, source, landing, source_sem, landing_sem)
    owner, local = place_of(source[...], row_groups)
    mine = owner == lax.axis_index("prow")
    wanted = as_column(jnp.where(mine, local, -1))
    chosen = (wanted == iota((NB, matrix.shape[0]), 1)).astype(BF16)
    rows[...] = dot(chosen, matrix[...]).astype(BF16)
    from_top = as_column(jnp.where(mine, landing[...], -1)) == iota((NB, NB), 1)
    place[...] = jnp.max(jnp.where(from_top, wanted, -1), axis=0, keepdims=True)


def pieces(x):
    high = x.astype(BF16)
    rest = x - high.astype(F32)
    middle = rest.astype(BF16)
    return high, middle, (rest - middle.astype(F32)).astype(BF16)


def invert_kernel(block, inverse):
    rows, cols = iota((HALF, HALF), 0), iota((HALF, HALF), 1)
    apart = rows ^ cols
    none = jnp.zeros((), BF16)
    halves = [slice(0, HALF), slice(HALF, NB)]
    lowers = [jnp.where(rows > cols, block[part, part], none) for part in halves]

    def corner(lower, size):
        return jnp.where((apart >= size) & (apart < 2 * size), lower, none)

    found = [jnp.where(rows == cols, 1.0, 0.0) - corner(lower, 1).astype(F32) for lower in lowers]
    size = 2
    while size < HALF:
        for i, lower in enumerate(lowers):
            x, edge = found[i], corner(lower, size)
            high, middle, low = pieces(x)
            first, second, third = pieces((dot(edge, low) + dot(edge, middle)) + dot(edge, high))
            small = (dot(high, third) + dot(low, first)) + dot(middle, second)
            found[i] = x - ((small + (dot(high, second) + dot(middle, first))) + dot(high, first))
        size *= 2
    for part, x in zip(halves, found):
        inverse[part] = x


def finish_kernel(n_parts, swaps, *refs):
    matrix, mine, passed, place, block, inverse, gather = refs[:7]
    parts, arrived = refs[7 : 7 + n_parts], refs[7 + n_parts : -7]
    out, made, left, keep, upper, load_sems, store_sems = refs[-7:]
    row_me, col_me = lax.axis_index("prow"), lax.axis_index("pcol")
    height, width = made.shape
    loads = []
    for i in range(height // NB):
        part = pl.ds(i * NB, NB)
        loads.append(pltpu.make_async_copy(matrix.at[part], made.at[part], load_sems.at[i]))
        loads[-1].start()

    @pl.when(col_me % 2 == 0)
    def _():
        left[:, :NB] = -mine[:height]

    @pl.when(col_me % 2 == 1)
    def _():
        left[:, :NB] = -passed[:height]

    hit = (iota((height, place.shape[1]), 0) == place[...]).astype(BF16)
    left[:, NB:] = hit[:, :swaps]
    gone = dot(hit, jnp.ones((place.shape[1], HALF), BF16))
    keep[...] = (1.0 - gone).astype(BF16)

    @pl.when(row_me == 0)
    def _():
        keep[:NB] = jnp.zeros((NB, HALF), BF16)
        left[:NB, :NB] = (iota((NB, NB), 0) == iota((NB, NB), 1)).astype(BF16)
        left[:NB, NB:] = jnp.zeros((NB, swaps), BF16)

    rows = jnp.concatenate([part[...] for part in parts], 0)
    top = dot(gather[...], rows)
    top1 = top[:HALF].astype(BF16)
    first = jnp.concatenate(pieces(inverse[:HALF]), 1)
    upper1 = dot(first, jnp.concatenate([top1] * 3, 0))
    edge = block[HALF:, :HALF]
    edges = jnp.concatenate([edge, edge, edge], 1)
    rest = top[HALF:] - dot(edges, jnp.concatenate(pieces(upper1), 0))
    x, y, z = pieces(inverse[HALF:])
    high, middle, low = pieces(rest)
    second = jnp.concatenate([x, x, y, y, x, z], 1)
    upper[:HALF] = upper1.astype(BF16)
    upper[HALF:NB] = dot(second, jnp.concatenate([high, middle, high, middle, low, high], 0)).astype(BF16)
    moved = arrived[0][...]
    for other in arrived[1:]:
        moved = moved + other[...]
    upper[NB:] = moved

    for load in loads:
        load.wait()
    stores = []
    for j in range(width // NB):
        cols = slice(j * NB, (j + 1) * NB)

        def compute(cols=cols):
            change = dot(left[...], upper[:, cols])
            kept = made[:, cols] * jnp.concatenate([keep[...], keep[...]], 1)
            made[:, cols] = (kept.astype(F32) + change).astype(BF16)

        if j == 0:
            pl.when(col_me != 0)(compute)
        else:
            compute()
        stores.append(pltpu.make_async_copy(made.at[:, cols], out.at[:, cols], store_sems.at[j]))
        stores[-1].start()
    for store in stores:
        store.wait()


SHAPE = jax.ShapeDtypeStruct
WHOLE = pl.BlockSpec(memory_space=pltpu.VMEM)


def params(limit=16):
    return pltpu.CompilerParams(vmem_limit_bytes=limit << 20)


def cost(flops=0, nbytes=0):
    return pl.CostEstimate(flops=flops, bytes_accessed=nbytes, transcendentals=0)


def finish(matrix, panel, passed, place, block, inverse, gather, parts, arrived):
    height, width = matrix.shape
    swaps = arrived[0].shape[0]
    return pl.pallas_call(
        functools.partial(finish_kernel, len(parts), swaps),
        out_shape=SHAPE(matrix.shape, BF16),
        in_specs=[pl.BlockSpec(memory_space=pl.ANY)] + [WHOLE] * (6 + len(parts) + len(arrived)),
        out_specs=pl.BlockSpec(memory_space=pl.ANY),
        scratch_shapes=[
            pltpu.VMEM((height, width), BF16),
            pltpu.VMEM((height, NB + swaps), BF16),
            pltpu.VMEM((height, HALF), BF16),
            pltpu.VMEM((NB + swaps, width), BF16),
            pltpu.SemaphoreType.DMA((height // NB,)),
            pltpu.SemaphoreType.DMA((width // NB,)),
        ],
        compiler_params=params(20),
        name="finish",
    )(matrix, panel, passed, place, block, inverse, gather, *parts, *arrived)


def spread(value, axes, index, count):
    step = count // 2
    while step:
        pairs = [(i, i + step) for i in range(0, count, 2 * step)]
        received = lax.ppermute(value, axes, pairs)
        value = jnp.where(lax.rem(index, 2 * step) == step, received, value)
        step //= 2
    return value


def two_rounds(row_groups):
    outer, inner = grid_of(row_groups)

    def hops(pair):
        a, b = pair
        return abs(a // inner - b // inner) + abs(a % inner - b % inner)

    count = 0
    while (count + 1) ** 2 < row_groups:
        count += 1
    holders = [0, outer // 2 * inner]
    holders += [i for i in range(row_groups) if i not in holders][: count - 1]
    left = [i for i in range(row_groups) if i not in holders]
    second = []
    while left:
        pairs, free = [], list(holders)
        while free and left:
            best = min(((a, b) for a in free for b in left), key=hops)
            pairs.append(best)
            free.remove(best[0])
            left.remove(best[1])
        second.append(pairs)
    return [[(0, i)] for i in holders[1:]], second


def local(matrix, pivots):
    height, width = matrix.shape
    row_groups, col_groups = lax.axis_size("prow"), lax.axis_size("pcol")
    row_me, col_me = lax.axis_index("prow"), lax.axis_index("pcol")
    outer, inner = grid_of(row_groups)
    cap = round_rows(row_groups)
    smem = pl.BlockSpec(memory_space=pltpu.SMEM)

    rows_out = [SHAPE((1, NB), I32), SHAPE((1, NB), I32)]
    swap_scratch = [
        pltpu.SMEM((height * row_groups,), I32),
        pltpu.SMEM((1, NB), I32),
        pltpu.SMEM((1, NB), I32),
        pltpu.SemaphoreType.DMA,
        pltpu.SemaphoreType.DMA,
    ]
    rows, source, landing, *gives = pl.pallas_call(
        functools.partial(pick_kernel, row_groups, cap),
        out_shape=[SHAPE((cap, width), BF16)] + rows_out + [SHAPE((outer * cap, width), BF16)] * inner,
        in_specs=[smem, pl.BlockSpec(memory_space=pl.ANY)],
        out_specs=[WHOLE] * (3 + inner),
        scratch_shapes=[pltpu.VMEM((height, width), BF16)]
        + swap_scratch
        + [pltpu.SemaphoreType.DMA((height // NB,))],
        compiler_params=params(16),
        cost_estimate=cost(2 * 4 * cap * width * height, 20 << 20),
        name="pick",
    )(pivots, matrix)
    gather, place, flag = pl.pallas_call(
        functools.partial(tables_kernel, row_groups, cap),
        out_shape=[SHAPE((NB, row_groups * cap), BF16), SHAPE((1, HALF), I32), SHAPE((1, HALF), I32)],
        in_specs=[WHOLE] * 2,
        out_specs=[WHOLE] * 3,
        compiler_params=params(),
        cost_estimate=cost(1 << 35, 32 << 20),
        name="tables",
    )(source, landing)

    both = ("prow", "pcol")
    me = row_me * col_groups + col_me
    first_round, second_round = two_rounds(row_groups)

    def send(value, rounds):
        for pairs in rounds:
            yield pairs, lax.ppermute(value, both, [(a * col_groups, b * col_groups) for a, b in pairs])

    def take(value, received):
        for pairs, other in received:
            takes = functools.reduce(jnp.logical_or, [me == b * col_groups for _, b in pairs])
            value = jnp.where(takes, other, value)
        return value

    def at(o, i):
        return o % outer * inner + i % inner

    everyone = [(o, i) for o in range(outer) for i in range(inner)]

    block = matrix[:NB, :NB]
    received = list(send(block, first_round))

    parts = [rows]
    for step in range(1, outer):
        parts.append(lax.ppermute(rows, "prow", [(at(o, i), at(o + step, i)) for o, i in everyone]))
    bundles = [lax.ppermute(gives[j], "prow", [(0, j)]) for j in range(1, inner)]
    arrays, _ = lax.optimization_barrier(([other for _, other in received], place))
    block = take(block, [(pairs, other) for (pairs, _), other in zip(received, arrays)])
    block = take(block, list(send(block, second_round)))
    panel = jnp.concatenate([matrix[:, :NB], block], 0)
    half = col_groups // 2
    hop = lax.ppermute(panel, "pcol", [(0, half)])
    gathered, *sent = pl.pallas_call(
        functools.partial(turn_kernel, row_groups, cap),
        out_shape=[SHAPE((outer * cap, width), BF16)] + [SHAPE((cap, width), BF16)] * outer,
        in_specs=[WHOLE] * (outer + inner),
        out_specs=[WHOLE] * (1 + outer),
        compiler_params=params(8),
        name="turn",
    )(*parts, gives[0], *bundles)

    hop, _ = lax.optimization_barrier((hop, (parts[-1], bundles)))
    panel = jnp.where(col_me == half, hop, panel)
    step = half // 2
    while step > 1:
        received = lax.ppermute(panel, "pcol", [(i, i + step) for i in range(0, col_groups, 2 * step)])
        panel = jnp.where(lax.rem(col_me, 2 * step) == step, received, panel)
        step //= 2

    parts = [gathered]
    for turn in range(1, inner):
        parts.append(lax.ppermute(gathered, "prow", [(at(o, i), at(o, i + turn)) for o, i in everyone]))
    arrived = [sent[0]]
    for step in range(1, outer):
        arrived.append(lax.ppermute(sent[step], "prow", [(i, at(step, i)) for i in range(inner)]))
    passed = lax.ppermute(panel, "pcol", [(i, i + 1) for i in range(0, col_groups, 2)])
    block = jnp.where(lax.rem(col_me, 2) == 1, passed[height:], panel[height:])
    inverse = pl.pallas_call(
        invert_kernel,
        out_shape=SHAPE((NB, HALF), F32),
        in_specs=[WHOLE],
        out_specs=WHOLE,
        cost_estimate=cost(2 * 60 * NB * NB * NB),
        name="invert",
    )(block)
    result = finish(matrix, panel, passed, place, block, inverse, gather, parts, arrived)

    def again(state):
        picked, place_all = pl.pallas_call(
            functools.partial(pick_all_kernel, row_groups),
            out_shape=[SHAPE((NB, width), BF16), SHAPE((1, NB), I32)],
            in_specs=[smem, WHOLE],
            out_specs=[WHOLE] * 2,
            scratch_shapes=[pltpu.VMEM((1, NB), I32)] * 2 + swap_scratch,
            compiler_params=params(),
            name="pick_all",
        )(pivots, matrix)
        top = picked
        for shift in range(1, row_groups):
            top = top + lax.ppermute(picked, "prow", [(i, (i + shift) % row_groups) for i in range(row_groups)])
        same = (iota((NB, NB), 0) == iota((NB, NB), 1)).astype(BF16)
        old_top = spread(matrix[:NB], "prow", row_me, row_groups)
        again_made = finish(matrix, panel, passed, place_all, block, inverse, same, [top], [old_top])
        return jnp.zeros((), jnp.bool_), again_made

    return lax.while_loop(lambda state: state[0], again, (flag[0, 0] > cap, result))[1]


def solution(mesh):
    placed = (P("prow", "pcol"), P())
    return jax.shard_map(
        local, mesh=mesh, in_specs=placed, out_specs=P("prow", "pcol"), check_vma=False
    )
```
